32 devices in a mesh: groups: 2 (over y), dp: 4 (over z), tensor: 4 (over x, core).
Axes of the slice: x: 2, y: 2, z: 4, core: 2. Of those that a mesh axis runs over, the one named last changes fastest.
Arguments:
- train_acts: bfloat16 [2048, 28672], P(('groups', 'dp'), 'tensor'), parts along dimension 0, may hold values from -6 to 6
- train_grads: bfloat16 [2048, 8192], P(('groups', 'dp'), 'tensor'), parts along dimension 0, may hold values from -6 to 6
- train_lengths: int32 [16], P(('groups', 'dp')), parts along dimension 0, may hold values from 32 to 128, as said below
- proj_in: bfloat16 [28672, 64], P('tensor'), may hold values from -0.03125 to 0.03125
- proj_out: bfloat16 [8192, 64], P('tensor'), may hold values from -0.0625 to 0.0625
- query_sketch: float32 [512, 4096], P(('groups', 'dp')), parts along dimension 0, may hold values from -6 to 6
- precond_in: float32 [64, 64], replicated
- precond_out: float32 [64, 64], replicated
Outputs:
- scores: float32 [16, 256], P(('groups', 'dp')), parts along dimension 0
The draws below stay inside these ranges and needn't reach their ends.
There are 2 independent parts, one for each index of `groups`. The reference program is written for one: setup_inputs(seed, part) draws one part's arguments, and reference() takes and returns one part's arrays. A program takes and returns all parts, laid end to end along the dimension named above; an argument that names none is the same for every part. Nothing has to cross between parts.
Inputs may be any that keep to these rules, and one draw needn't show every extreme that they name: `train_lengths`: each training sequence has at least 32 valid tokens; some sequence has all 128.
All inputs are finite; a program needn't handle non-finite values.
Results may differ from the reference program's by a relative error of at most 0.0003.
Values sent between devices are 32-bit elements; how exact they have to be, the bound alone decides.
A program may use at most 64 MiB of HBM per device.

```python
import math
import jax
import jax.numpy as jnp
from jax import lax

D = 8192
FF = 28672
RANK_IN = 64
RANK_OUT = 64
SEQ = 128
TRAIN = 8
QUERIES = 256
TRAIN_TOK = 1024


def factor_matrix(key, width):
    first, second = jax.random.split(key)
    diag_part = jnp.exp(jax.random.uniform(first, (width,), jnp.float32, jnp.log(0.5), jnp.log(2.0)))
    spread = jax.random.normal(second, (width, width), jnp.float32) * (0.3 / jnp.sqrt(jnp.float32(width)))
    return (jnp.diag(diag_part) + spread).astype(jnp.float32)


def draw_train_lengths(key, part):
    key = jax.random.fold_in(key, 11)
    first, second = jax.random.split(key)
    values = jax.random.randint(first, (TRAIN,), SEQ // 4, SEQ + 1)
    place = jax.random.randint(second, (), 0, TRAIN)
    return jnp.where(jnp.arange(TRAIN) == place, SEQ, values).astype(jnp.int32)


def draw_precond_in(key, part):
    key = jax.random.fold_in(key, 23)
    return factor_matrix(key, RANK_IN)


def draw_precond_out(key, part):
    key = jax.random.fold_in(key, 37)
    return factor_matrix(key, RANK_OUT)


def block_scale(stream_key, extent, cuts, low, largest):
    level = 1.0
    for axis_at, shards_of in cuts:
        heights = jax.random.uniform(jax.random.fold_in(jax.random.fold_in(stream_key, 6), axis_at), (shards_of,), jnp.float32, low / len(cuts), largest / len(cuts))
        level = level * jnp.repeat(jnp.exp(heights), extent[axis_at] // shards_of).reshape((-1,) + (1,) * (len(extent) - 1 - axis_at))
    return level


def noise(own_key, extent, deviation, most, cuts=(), kind=jnp.bfloat16):
    drawn = jax.random.normal(own_key, extent, jnp.float32) * deviation
    if len(cuts) > 0:
        drawn = block_scale(own_key, extent, cuts, -0.22, 0.18) * drawn
    return jnp.clip(drawn, min=-most, max=most).astype(kind)


def setup_inputs(seed: int = 0, part: int = 0) -> dict:
    key_list = jax.random.split(jax.random.key(seed), 9)
    own_keys = jax.random.split(jax.random.fold_in(key_list[8], part), 9)
    train_acts = noise(own_keys[0], (TRAIN_TOK, FF), 1.0, 6.0, ((0, 4), (1, 4)))
    train_grads = noise(own_keys[1], (TRAIN_TOK, D), 1.0, 6.0, ((0, 4), (1, 4)))
    train_lengths = draw_train_lengths(jax.random.fold_in(jax.random.fold_in(key_list[8], part), 71), part)
    proj_in = noise(key_list[3], (FF, RANK_IN), FF ** -0.5, 0.03125, ((0, 4),))
    proj_out = noise(key_list[4], (D, RANK_OUT), D ** -0.5, 0.0625, ((0, 4),))
    query_sketch = noise(own_keys[5], (QUERIES, RANK_IN * RANK_OUT), 1.0, 6.0, ((0, 4),), jnp.float32)
    precond_in = draw_precond_in(jax.random.fold_in(key_list[8], 71), part)
    precond_out = draw_precond_out(jax.random.fold_in(key_list[8], 71), part)
    return {"train_acts": train_acts, "train_grads": train_grads, "train_lengths": train_lengths, "proj_in": proj_in, "proj_out": proj_out, "query_sketch": query_sketch, "precond_in": precond_in, "precond_out": precond_out}


def reference(train_acts, train_grads, train_lengths, proj_in, proj_out, query_sketch, precond_in, precond_out):
    left_proj = jnp.dot(train_acts, proj_in, preferred_element_type=jnp.float32)
    right_proj = jnp.dot(train_grads, proj_out, preferred_element_type=jnp.float32)
    count = train_lengths.shape[0]
    slots = jnp.arange(SEQ, dtype=jnp.int32)
    keep = (slots[None, :] < train_lengths[:, None]).astype(jnp.float32)
    left_seq = left_proj.reshape(count, SEQ, RANK_IN) * keep[:, :, None]
    right_seq = right_proj.reshape(count, SEQ, RANK_OUT)
    sketch = jnp.einsum('sti,stj->sij', left_seq, right_seq, precision=lax.Precision.HIGHEST)
    sketch = sketch * jnp.float32(1.0 / math.sqrt(SEQ))
    flat_sketch = sketch.reshape(count, RANK_IN * RANK_OUT)
    raw = query_sketch.reshape(QUERIES, RANK_IN, RANK_OUT)
    leftmul = jnp.einsum('ik,nkl->nil', precond_in, raw, precision=lax.Precision.HIGHEST)
    cond = jnp.einsum('nil,lj->nij', leftmul, precond_out, precision=lax.Precision.HIGHEST)
    cond = cond.reshape(QUERIES, RANK_IN * RANK_OUT)
    scores = lax.dot_general(flat_sketch, cond, (((1,), (1,)), ((), ())), precision=lax.Precision.HIGHEST)
    return scores * jnp.float32(1.0 / math.sqrt(RANK_IN * RANK_OUT))
```

```python
import functools
import math

import jax
import jax.numpy as jnp
from jax import lax
from jax.experimental import pallas as pl
from jax.experimental.pallas import tpu as pltpu
from jax.sharding import PartitionSpec as P

HIGH = lax.Precision.HIGHEST
MESH = pl.DeviceIdType.MESH
NT = (((1,), (1,)), ((), ()))
NN = (((1,), (0,)), ((), ()))


def f32dot(a, b, dims):
    return lax.dot_general(a, b, dims, precision=HIGH, preferred_element_type=jnp.float32)


def bf16dot(a, b):
    return lax.dot_general(a, b, NT, preferred_element_type=jnp.float32)


def loop(low, high, body):
    if high - low <= 4:
        for i in range(low, high):
            body(i)
    else:
        def step(i, carry):
            body(i)
            return carry
        lax.fori_loop(low, high, step, 0)


def kernel(
    nd, nt, seq_len, scale,
    lengths, acts, grads, pin, pout, query, pre_in, pre_out,
    out,
    acts_v, grads_v, pin_v, pout_v, query_v, pre_in_v, pre_out_v,
    part, got, gather, rows, final,
    load_sem, send_a, recv_a, send_b, recv_b, send_c, recv_c,
):
    d = lax.axis_index("dp")
    t = lax.axis_index("tensor")
    width = pin.shape[0]
    half = width // 2
    tok = acts.shape[0] // nt
    count = out.shape[0]
    nq = query.shape[0]
    total = nd * nt

    def place(k):
        chips = nt // 2
        return ((t // 2 + chips - 1 - k // 2) % chips) * 2 + (t % 2 + 1 - k % 2) % 2

    fixed = [
        pltpu.make_async_copy(src, dst, load_sem.at[2 * nt + i])
        for i, (src, dst) in enumerate(
            [(pre_in, pre_in_v), (pre_out, pre_out_v), (pin, pin_v), (pout, pout_v), (query, query_v)]
        )
    ]
    for copy in fixed[:4]:
        copy.start()
    loads = []
    for k in range(nt):
        chunk = pl.ds(pl.multiple_of(place(k) * tok, tok), tok)
        loads.append((
            pltpu.make_async_copy(acts.at[chunk, :], acts_v.at[k], load_sem.at[2 * k]),
            pltpu.make_async_copy(grads.at[chunk, :], grads_v.at[k], load_sem.at[2 * k + 1]),
        ))
        for copy in loads[k]:
            copy.start()
    fixed[4].start()

    barrier = pltpu.get_barrier_semaphore()

    def greet(i):
        other = (d * nt + t + i) % total
        pl.semaphore_signal(
            barrier, inc=1, device_id={"dp": other // nt, "tensor": other % nt}, device_id_type=MESH
        )

    if total <= 16:
        for i in range(1, total):
            greet(i)
    else:
        loop(1, total, greet)

    for copy in fixed[:2]:
        copy.wait()
    r = lax.broadcasted_iota(jnp.int32, (width, width), 0)
    c = lax.broadcasted_iota(jnp.int32, (width, width), 1)
    pick = jnp.where(c == jnp.where(r < half, 2 * r, 2 * (r - half) + 1), 1.0, 0.0).astype(jnp.float32)
    pre_t = f32dot(pick, pre_in_v[...], NT)

    for copy in fixed[2:4]:
        copy.wait()
    sends = []
    for k in range(nt):
        for copy in loads[k]:
            copy.wait()
        part[k, 0:width, 0:tok] = bf16dot(pin_v[...], acts_v[k])
        part[k, 0:tok, tok : tok + width] = bf16dot(grads_v[k], pout_v[...])
        if k == 0:
            pl.semaphore_wait(barrier, total - 1)
        if k < nt - 1:
            copy = pltpu.make_async_remote_copy(
                src_ref=part.at[k], dst_ref=got.at[k], send_sem=send_a.at[k], recv_sem=recv_a.at[k],
                device_id={"tensor": place(k)}, device_id_type=MESH,
            )
            copy.start()
            sends.append(copy)
    fixed[4].wait()

    left = part[nt - 1, 0:width, 0:tok]
    right = part[nt - 1, 0:tok, tok : tok + width]
    for k in range(nt - 2, -1, -1):
        sends[k].wait_recv()
        left = left + got[k, 0:width, 0:tok]
        right = right + got[k, 0:tok, tok : tok + width]
    start = t * tok
    length = lengths[start // seq_len]
    slot = lax.broadcasted_iota(jnp.int32, (width, tok), 1) + start % seq_len
    left = jnp.where(slot < length, left, 0.0)
    u = f32dot(pre_t, left, NN)
    w = f32dot(right, pre_out_v[...], NT)
    g = f32dot(u, w, NN)
    gather[0] = jnp.concatenate([g[:half], g[half:]], axis=1)

    def gather_copy(j):
        return pltpu.make_async_remote_copy(
            src_ref=gather.at[0], dst_ref=gather.at[j], send_sem=send_b.at[j], recv_sem=recv_b.at[j],
            device_id={"dp": (d + j) % nd}, device_id_type=MESH,
        )

    loop(1, nd, lambda j: gather_copy(j).start())

    ones = jnp.ones((8, 2 * width), jnp.float32)
    mine = d * nt + t

    def score(j):
        acc = jnp.zeros((nq, 2 * width), jnp.float32)
        for p in range(half):
            acc = acc + query_v[:, 2 * width * p : 2 * width * (p + 1)] * gather[j, p : p + 1, :]
        row = f32dot(ones, acc, NT)[0:1] * scale
        rows[j] = jnp.concatenate([row, row], axis=1)

    def row_copy(j, to):
        return pltpu.make_async_remote_copy(
            src_ref=rows.at[j], dst_ref=final.at[mine], send_sem=send_c, recv_sem=recv_c,
            device_id={"dp": (d + nd - j) % nd, "tensor": to}, device_id_type=MESH,
        )

    score(0)
    final[mine] = rows[0]
    loop(1, nt, lambda k: row_copy(0, (t + k) % nt).start())

    def step(j):
        gather_copy(j).wait_recv()
        score(j)
        loop(0, nt, lambda k: row_copy(j, (t + k) % nt).start())

    loop(1, nd, step)

    for copy in sends:
        copy.wait_send()
    loop(1, nd, lambda j: gather_copy(j).wait_send())
    most = final.at[pl.ds(0, total - 1)]
    pltpu.make_async_copy(most, most, send_c).wait()
    pltpu.make_async_copy(most, most, recv_c).wait()

    share = nt // count
    lane = lax.broadcasted_iota(jnp.int32, (1, 2 * nq), 1)
    for s in range(count):
        for pair in range(nd // 2):
            sums = []
            for e in range(2):
                base = (2 * pair + e) * nt + s * share
                value = final[base]
                for i in range(1, share):
                    value = value + final[base + i]
                sums.append(value)
            out[s : s + 1, 2 * nq * pair : 2 * nq * (pair + 1)] = jnp.where(lane < nq, sums[0], sums[1])


def solution(mesh):
    nd, nt = mesh.shape["dp"], mesh.shape["tensor"]

    def local(acts, grads, lengths, pin, pout, query, pre_in, pre_out):
        tokens, deep_in = acts.shape
        deep_out = grads.shape[1]
        count = lengths.shape[0]
        width = pin.shape[1]
        nq = query.shape[0]
        tok = tokens // nt
        seq_len = tokens // count
        scale = 1.0 / math.sqrt(seq_len) / math.sqrt(width * width)
        box = (max(width, tok), tok + width)
        anywhere = pl.BlockSpec(memory_space=pltpu.HBM)
        f32 = jnp.float32
        dma = pltpu.SemaphoreType.DMA
        return pl.pallas_call(
            functools.partial(kernel, nd, nt, seq_len, scale),
            out_shape=jax.ShapeDtypeStruct((count, nd * nq), f32),
            in_specs=[pl.BlockSpec(memory_space=pltpu.SMEM)] + [anywhere] * 7,
            out_specs=pl.BlockSpec(memory_space=pltpu.VMEM),
            scratch_shapes=[
                pltpu.VMEM((nt, tok, deep_in), acts.dtype),
                pltpu.VMEM((nt, tok, deep_out), grads.dtype),
                pltpu.VMEM((width, deep_in), pin.dtype),
                pltpu.VMEM((width, deep_out), pout.dtype),
                pltpu.VMEM(query.shape, f32),
                pltpu.VMEM(pre_in.shape, f32),
                pltpu.VMEM(pre_out.shape, f32),
                pltpu.VMEM((nt,) + box, f32),
                pltpu.VMEM((nt - 1,) + box, f32),
                pltpu.VMEM((nd, width // 2, 2 * width), f32),
                pltpu.VMEM((nd, 1, 2 * nq), f32),
                pltpu.VMEM((nd * nt, 1, 2 * nq), f32),
                dma((2 * nt + 5,)), dma((nt - 1,)), dma((nt - 1,)), dma((nd,)), dma((nd,)), dma, dma,
            ],
            compiler_params=pltpu.CompilerParams(
                collective_id=0, has_side_effects=True, vmem_limit_bytes=48 * 1024 * 1024
            ),
        )(lengths, acts, grads, pin.T, pout.T, query, pre_in, pre_out)

    placed = (
        P(("groups", "dp"), "tensor"),
        P(("groups", "dp"), "tensor"),
        P(("groups", "dp")),
        P("tensor", None),
        P("tensor", None),
        P(("groups", "dp"), None),
        P(),
        P(),
    )
    return jax.shard_map(
        local, mesh=mesh, in_specs=placed, out_specs=P(("groups", "dp"), None), check_vma=False
    )
```

```python
import functools
import math

import jax
import jax.numpy as jnp
from jax import lax
from jax.experimental import pallas as pl
from jax.experimental.pallas import tpu as pltpu
from jax.sharding import PartitionSpec as P

HIGH = lax.Precision.HIGHEST
MESH = pl.DeviceIdType.MESH
NT = (((1,), (1,)), ((), ()))
NN = (((1,), (0,)), ((), ()))


def f32dot(a, b, dims):
    return lax.dot_general(a, b, dims, precision=HIGH, preferred_element_type=jnp.float32)


def halves(a):
    high = a.astype(jnp.bfloat16)
    return high, (a - high.astype(jnp.float32)).astype(jnp.bfloat16)


def split_dot(a, b, dims):
    (ah, al), (bh, bl) = halves(a), halves(b)
    return (
        lax.dot_general(ah, bh, dims, preferred_element_type=jnp.float32)
        + lax.dot_general(ah, bl, dims, preferred_element_type=jnp.float32)
        + lax.dot_general(al, bh, dims, preferred_element_type=jnp.float32)
    )


def bf16dot(a, b):
    return lax.dot_general(a, b, NT, preferred_element_type=jnp.float32)


def loop(low, high, body):
    if high - low <= 4:
        for i in range(low, high):
            body(i)
    else:
        def step(i, carry):
            body(i)
            return carry
        lax.fori_loop(low, high, step, 0)


def kernel(
    nd, nt, seq_len, scale,
    lengths, acts, grads, pin, pout, query, pre_in, pre_out,
    out,
    acts_v, grads_v, pin_v, pout_v, query_v, pre_in_v, pre_out_v,
    part, got, gather, rows, final,
    load_sem, send_a, recv_a, send_b, recv_b, send_c, recv_c,
):
    d = lax.axis_index("dp")
    t = lax.axis_index("tensor")
    width = pin.shape[0]
    half = width // 2
    tok = acts.shape[0] // nt
    count = out.shape[0]
    nq = query.shape[0]
    total = nd * nt

    def place(k):
        chips = nt // 2
        return ((t // 2 + chips - 1 - k // 2) % chips) * 2 + (t % 2 + 1 - k % 2) % 2

    barrier = pltpu.get_barrier_semaphore()

    def greet(name, place, size):
        def one(i):
            pl.semaphore_signal(barrier, inc=1, device_id={name: (place + i) % size}, device_id_type=MESH)
        loop(1, size, one)

    greet("dp", d, nd)
    greet("tensor", t, nt)

    fixed = [
        pltpu.make_async_copy(src, dst, load_sem.at[2 * nt + i])
        for i, (src, dst) in enumerate(
            [(pre_in, pre_in_v), (pre_out, pre_out_v), (pin, pin_v), (pout, pout_v), (query, query_v)]
        )
    ]
    for copy in fixed[:4]:
        copy.start()
    loads = []
    for k in range(nt):
        chunk = pl.ds(pl.multiple_of(place(k) * tok, tok), tok)
        loads.append((
            pltpu.make_async_copy(acts.at[chunk, :], acts_v.at[k], load_sem.at[2 * k]),
            pltpu.make_async_copy(grads.at[chunk, :], grads_v.at[k], load_sem.at[2 * k + 1]),
        ))
        for copy in loads[k]:
            copy.start()
    fixed[4].start()

    for copy in fixed[:2]:
        copy.wait()
    r = lax.broadcasted_iota(jnp.int32, (width, width), 0)
    c = lax.broadcasted_iota(jnp.int32, (width, width), 1)
    pick = jnp.where(c == jnp.where(r < half, 2 * r, 2 * (r - half) + 1), 1.0, 0.0).astype(jnp.float32)
    pre_t = f32dot(pick, pre_in_v[...], NT)

    for copy in fixed[2:4]:
        copy.wait()
    sends = []
    for k in range(nt):
        for copy in loads[k]:
            copy.wait()
        part[k, 0:width, 0:tok] = bf16dot(pin_v[...], acts_v[k])
        part[k, 0:tok, tok : tok + width] = bf16dot(grads_v[k], pout_v[...])
    pl.semaphore_wait(barrier, nd + nt - 2)
    for k in range(nt - 1):
        copy = pltpu.make_async_remote_copy(
            src_ref=part.at[k], dst_ref=got.at[k], send_sem=send_a.at[k], recv_sem=recv_a.at[k],
            device_id={"tensor": place(k)}, device_id_type=MESH,
        )
        copy.start()
        sends.append(copy)
    fixed[4].wait()

    left = part[nt - 1, 0:width, 0:tok]
    right = part[nt - 1, 0:tok, tok : tok + width]
    for k in range(nt - 2, -1, -1):
        sends[k].wait_recv()
        left = left + got[k, 0:width, 0:tok]
        right = right + got[k, 0:tok, tok : tok + width]
    start = t * tok
    length = lengths[start // seq_len]
    slot = lax.broadcasted_iota(jnp.int32, (width, tok), 1) + start % seq_len
    left = jnp.where(slot < length, left, 0.0)
    u = split_dot(pre_t, left, NN)
    w = split_dot(right, pre_out_v[...], NT)
    g = split_dot(u, w, NN)
    gather[0] = jnp.concatenate([g[:half], g[half:]], axis=1)

    def gather_copy(j):
        return pltpu.make_async_remote_copy(
            src_ref=gather.at[0], dst_ref=gather.at[j], send_sem=send_b.at[j], recv_sem=recv_b.at[j],
            device_id={"dp": (d + j) % nd}, device_id_type=MESH,
        )

    loop(1, nd, lambda j: gather_copy(j).start())

    ones = jnp.ones((8, 2 * width), jnp.bfloat16)
    mine = d * nt + t

    def score(j):
        acc = jnp.zeros((nq, 2 * width), jnp.float32)
        for p in range(half):
            acc = acc + query_v[:, 2 * width * p : 2 * width * (p + 1)] * gather[j, p : p + 1, :]
        high, low = halves(acc)
        row = (bf16dot(ones, high) + bf16dot(ones, low))[0:1] * scale
        rows[j] = jnp.concatenate([row, row], axis=1)

    def row_copy(j, to):
        return pltpu.make_async_remote_copy(
            src_ref=rows.at[j], dst_ref=final.at[mine], send_sem=send_c, recv_sem=recv_c,
            device_id={"dp": (d + nd - j) % nd, "tensor": to}, device_id_type=MESH,
        )

    score(0)
    final[mine] = rows[0]
    loop(1, nt, lambda k: row_copy(0, (t + k) % nt).start())

    def step(j):
        gather_copy(j).wait_recv()
        score(j)
        loop(0, nt, lambda k: row_copy(j, (t + k) % nt).start())

    loop(1, nd, step)

    for copy in sends:
        copy.wait_send()
    loop(1, nd, lambda j: gather_copy(j).wait_send())
    most = final.at[pl.ds(0, total - 1)]
    pltpu.make_async_copy(most, most, send_c).wait()
    pltpu.make_async_copy(most, most, recv_c).wait()

    share = nt // count
    lane = lax.broadcasted_iota(jnp.int32, (1, 2 * nq), 1)
    for s in range(count):
        for pair in range(nd // 2):
            sums = []
            for e in range(2):
                base = (2 * pair + e) * nt + s * share
                value = final[base]
                for i in range(1, share):
                    value = value + final[base + i]
                sums.append(value)
            out[s : s + 1, 2 * nq * pair : 2 * nq * (pair + 1)] = jnp.where(lane < nq, sums[0], sums[1])


def solution(mesh):
    nd, nt = mesh.shape["dp"], mesh.shape["tensor"]

    def local(acts, grads, lengths, pin, pout, query, pre_in, pre_out):
        tokens, deep_in = acts.shape
        deep_out = grads.shape[1]
        count = lengths.shape[0]
        width = pin.shape[1]
        nq = query.shape[0]
        tok = tokens // nt
        seq_len = tokens // count
        scale = 1.0 / math.sqrt(seq_len) / math.sqrt(width * width)
        box = (max(width, tok), tok + width)
        anywhere = pl.BlockSpec(memory_space=pltpu.HBM)
        f32 = jnp.float32
        dma = pltpu.SemaphoreType.DMA
        return pl.pallas_call(
            functools.partial(kernel, nd, nt, seq_len, scale),
            out_shape=jax.ShapeDtypeStruct((count, nd * nq), f32),
            in_specs=[pl.BlockSpec(memory_space=pltpu.SMEM)] + [anywhere] * 7,
            out_specs=pl.BlockSpec(memory_space=pltpu.VMEM),
            scratch_shapes=[
                pltpu.VMEM((nt, tok, deep_in), acts.dtype),
                pltpu.VMEM((nt, tok, deep_out), grads.dtype),
                pltpu.VMEM((width, deep_in), pin.dtype),
                pltpu.VMEM((width, deep_out), pout.dtype),
                pltpu.VMEM(query.shape, f32),
                pltpu.VMEM(pre_in.shape, f32),
                pltpu.VMEM(pre_out.shape, f32),
                pltpu.VMEM((nt,) + box, f32),
                pltpu.VMEM((nt - 1,) + box, f32),
                pltpu.VMEM((nd, width // 2, 2 * width), f32),
                pltpu.VMEM((nd, 1, 2 * nq), f32),
                pltpu.VMEM((nd * nt, 1, 2 * nq), f32),
                dma((2 * nt + 5,)), dma((nt - 1,)), dma((nt - 1,)), dma((nd,)), dma((nd,)), dma, dma,
            ],
            compiler_params=pltpu.CompilerParams(
                collective_id=0, has_side_effects=True, vmem_limit_bytes=60 * 1024 * 1024
            ),
        )(lengths, acts, grads, pin.T, pout.T, query, pre_in, pre_out)

    placed = (
        P(("groups", "dp"), "tensor"),
        P(("groups", "dp"), "tensor"),
        P(("groups", "dp")),
        P("tensor", None),
        P("tensor", None),
        P(("groups", "dp"), None),
        P(),
        P(),
    )
    return jax.shard_map(
        local, mesh=mesh, in_specs=placed, out_specs=P(("groups", "dp"), None), check_vma=False
    )
```

```python
import functools
import math

import jax
import jax.numpy as jnp
from jax import lax
from jax.experimental import pallas as pl
from jax.experimental.pallas import tpu as pltpu
from jax.sharding import PartitionSpec as P

HIGH = lax.Precision.HIGHEST
MESH = pl.DeviceIdType.MESH
NT = (((1,), (1,)), ((), ()))
NN = (((1,), (0,)), ((), ()))


def f32dot(a, b, dims):
    return lax.dot_general(a, b, dims, precision=HIGH, preferred_element_type=jnp.float32)


def halves(a):
    high = a.astype(jnp.bfloat16)
    return high, (a - high.astype(jnp.float32)).astype(jnp.bfloat16)


def split_dot(a, b, dims):
    (ah, al), (bh, bl) = halves(a), halves(b)
    return (
        lax.dot_general(ah, bh, dims, preferred_element_type=jnp.float32)
        + lax.dot_general(ah, bl, dims, preferred_element_type=jnp.float32)
        + lax.dot_general(al, bh, dims, preferred_element_type=jnp.float32)
    )


def bf16dot(a, b):
    return lax.dot_general(a, b, NT, preferred_element_type=jnp.float32)


def loop(low, high, body):
    if high - low <= 4:
        for i in range(low, high):
            body(i)
    else:
        def step(i, carry):
            body(i)
            return carry
        lax.fori_loop(low, high, step, 0)


def kernel(
    nd, nt, seq_len, scale,
    lengths, acts, grads, pin, pout, query, pre_in, pre_out,
    out,
    acts_v, grads_v, pin_v, pout_v, query_v, pre_in_v, pre_out_v,
    part, got, gather, rows, final,
    load_sem, send_a, recv_a, send_b, recv_b, send_c, recv_c,
):
    d = lax.axis_index("dp")
    t = lax.axis_index("tensor")
    width = pin.shape[0]
    half = width // 2
    tok = acts.shape[0] // nt
    count = out.shape[0]
    nq = query.shape[0]
    total = nd * nt

    def place(k):
        chips = nt // 2
        return ((t // 2 + chips - 1 - k // 2) % chips) * 2 + (t % 2 + 1 - k % 2) % 2

    barrier = pltpu.get_barrier_semaphore()

    def greet(name, place, size):
        def one(i):
            pl.semaphore_signal(barrier, inc=1, device_id={name: (place + i) % size}, device_id_type=MESH)
        loop(1, size, one)

    greet("dp", d, nd)
    greet("tensor", t, nt)

    fixed = [
        pltpu.make_async_copy(src, dst, load_sem.at[2 * nt + i])
        for i, (src, dst) in enumerate(
            [(pre_in, pre_in_v), (pre_out, pre_out_v), (pin, pin_v), (pout, pout_v), (query, query_v)]
        )
    ]
    for copy in fixed[:4]:
        copy.start()
    loads = []
    for k in range(nt):
        chunk = pl.ds(pl.multiple_of(place(k) * tok, tok), tok)
        loads.append((
            pltpu.make_async_copy(acts.at[chunk, :], acts_v.at[k], load_sem.at[2 * k]),
            pltpu.make_async_copy(grads.at[chunk, :], grads_v.at[k], load_sem.at[2 * k + 1]),
        ))
        for copy in loads[k]:
            copy.start()
    fixed[4].start()

    for copy in fixed[:2]:
        copy.wait()
    r = lax.broadcasted_iota(jnp.int32, (width, width), 0)
    c = lax.broadcasted_iota(jnp.int32, (width, width), 1)
    pick = jnp.where(c == jnp.where(r < half, 2 * r, 2 * (r - half) + 1), 1.0, 0.0).astype(jnp.float32)
    pre_t = f32dot(pick, pre_in_v[...], NT)

    for copy in fixed[2:4]:
        copy.wait()
    sends = []
    for k in range(nt):
        for copy in loads[k]:
            copy.wait()
        part[k, 0:width, 0:tok] = bf16dot(pin_v[...], acts_v[k])
        part[k, 0:tok, tok : tok + width] = bf16dot(grads_v[k], pout_v[...])
        if k == 0:
            pl.semaphore_wait(barrier, nd + nt - 2)
        if k < nt - 1:
            copy = pltpu.make_async_remote_copy(
                src_ref=part.at[k], dst_ref=got.at[k], send_sem=send_a.at[k], recv_sem=recv_a.at[k],
                device_id={"tensor": place(k)}, device_id_type=MESH,
            )
            copy.start()
            sends.append(copy)
    fixed[4].wait()

    left = part[nt - 1, 0:width, 0:tok]
    right = part[nt - 1, 0:tok, tok : tok + width]
    for k in range(nt - 2, -1, -1):
        sends[k].wait_recv()
        left = left + got[k, 0:width, 0:tok]
        right = right + got[k, 0:tok, tok : tok + width]
    start = t * tok
    length = lengths[start // seq_len]
    slot = lax.broadcasted_iota(jnp.int32, (width, tok), 1) + start % seq_len
    left = jnp.where(slot < length, left, 0.0)
    u = split_dot(pre_t, left, NN)
    w = split_dot(right, pre_out_v[...], NT)
    g = split_dot(u, w, NN)
    gather[0] = jnp.concatenate([g[:half], g[half:]], axis=1)

    def gather_copy(j):
        return pltpu.make_async_remote_copy(
            src_ref=gather.at[0], dst_ref=gather.at[j], send_sem=send_b.at[j], recv_sem=recv_b.at[j],
            device_id={"dp": (d + j) % nd}, device_id_type=MESH,
        )

    loop(1, nd, lambda j: gather_copy(j).start())

    ones = jnp.ones((8, 2 * width), jnp.bfloat16)
    mine = d * nt + t

    def score(j):
        acc = jnp.zeros((nq, 2 * width), jnp.float32)
        for p in range(half):
            acc = acc + query_v[:, 2 * width * p : 2 * width * (p + 1)] * gather[j, p : p + 1, :]
        high, low = halves(acc)
        row = (bf16dot(ones, high) + bf16dot(ones, low))[0:1] * scale
        rows[j] = jnp.concatenate([row, row], axis=1)

    def row_copy(j, to):
        return pltpu.make_async_remote_copy(
            src_ref=rows.at[j], dst_ref=final.at[mine], send_sem=send_c, recv_sem=recv_c,
            device_id={"dp": (d + nd - j) % nd, "tensor": to}, device_id_type=MESH,
        )

    score(0)
    final[mine] = rows[0]
    loop(1, nt, lambda k: row_copy(0, (t + k) % nt).start())

    def step(j):
        gather_copy(j).wait_recv()
        score(j)
        loop(0, nt, lambda k: row_copy(j, (t + k) % nt).start())

    loop(1, nd, step)

    for copy in sends:
        copy.wait_send()
    loop(1, nd, lambda j: gather_copy(j).wait_send())
    most = final.at[pl.ds(0, total - 1)]
    pltpu.make_async_copy(most, most, send_c).wait()
    pltpu.make_async_copy(most, most, recv_c).wait()

    share = nt // count
    lane = lax.broadcasted_iota(jnp.int32, (1, 2 * nq), 1)
    for s in range(count):
        for pair in range(nd // 2):
            sums = []
            for e in range(2):
                base = (2 * pair + e) * nt + s * share
                value = final[base]
                for i in range(1, share):
                    value = value + final[base + i]
                sums.append(value)
            out[s : s + 1, 2 * nq * pair : 2 * nq * (pair + 1)] = jnp.where(lane < nq, sums[0], sums[1])


def solution(mesh):
    nd, nt = mesh.shape["dp"], mesh.shape["tensor"]

    def local(acts, grads, lengths, pin, pout, query, pre_in, pre_out):
        tokens, deep_in = acts.shape
        deep_out = grads.shape[1]
        count = lengths.shape[0]
        width = pin.shape[1]
        nq = query.shape[0]
        tok = tokens // nt
        seq_len = tokens // count
        scale = 1.0 / math.sqrt(seq_len) / math.sqrt(width * width)
        box = (max(width, tok), tok + width)
        anywhere = pl.BlockSpec(memory_space=pltpu.HBM)
        f32 = jnp.float32
        dma = pltpu.SemaphoreType.DMA
        return pl.pallas_call(
            functools.partial(kernel, nd, nt, seq_len, scale),
            out_shape=jax.ShapeDtypeStruct((count, nd * nq), f32),
            in_specs=[pl.BlockSpec(memory_space=pltpu.SMEM)] + [anywhere] * 7,
            out_specs=pl.BlockSpec(memory_space=pltpu.VMEM),
            scratch_shapes=[
                pltpu.VMEM((nt, tok, deep_in), acts.dtype),
                pltpu.VMEM((nt, tok, deep_out), grads.dtype),
                pltpu.VMEM((width, deep_in), pin.dtype),
                pltpu.VMEM((width, deep_out), pout.dtype),
                pltpu.VMEM(query.shape, f32),
                pltpu.VMEM(pre_in.shape, f32),
                pltpu.VMEM(pre_out.shape, f32),
                pltpu.VMEM((nt,) + box, f32),
                pltpu.VMEM((nt - 1,) + box, f32),
                pltpu.VMEM((nd, width // 2, 2 * width), f32),
                pltpu.VMEM((nd, 1, 2 * nq), f32),
                pltpu.VMEM((nd * nt, 1, 2 * nq), f32),
                dma((2 * nt + 5,)), dma((nt - 1,)), dma((nt - 1,)), dma((nd,)), dma((nd,)), dma, dma,
            ],
            compiler_params=pltpu.CompilerParams(
                collective_id=0, has_side_effects=True, vmem_limit_bytes=60 * 1024 * 1024
            ),
        )(lengths, acts, grads, pin.T, pout.T, query, pre_in, pre_out)

    placed = (
        P(("groups", "dp"), "tensor"),
        P(("groups", "dp"), "tensor"),
        P(("groups", "dp")),
        P("tensor", None),
        P("tensor", None),
        P(("groups", "dp"), None),
        P(),
        P(),
    )
    return jax.shard_map(
        local, mesh=mesh, in_specs=placed, out_specs=P(("groups", "dp"), None), check_vma=False
    )
```

```python
import functools
import math

import jax
import jax.numpy as jnp
from jax import lax
from jax.experimental import pallas as pl
from jax.experimental.pallas import tpu as pltpu
from jax.sharding import PartitionSpec as P

HIGH = lax.Precision.HIGHEST
MESH = pl.DeviceIdType.MESH
NT = (((1,), (1,)), ((), ()))
NN = (((1,), (0,)), ((), ()))


def f32dot(a, b, dims):
    return lax.dot_general(a, b, dims, precision=HIGH, preferred_element_type=jnp.float32)


def halves(a):
    high = a.astype(jnp.bfloat16)
    return high, (a - high.astype(jnp.float32)).astype(jnp.bfloat16)


def split_dot(a, b, dims):
    (ah, al), (bh, bl) = halves(a), halves(b)
    return (
        lax.dot_general(ah, bh, dims, preferred_element_type=jnp.float32)
        + lax.dot_general(ah, bl, dims, preferred_element_type=jnp.float32)
        + lax.dot_general(al, bh, dims, preferred_element_type=jnp.float32)
    )


def bf16dot(a, b):
    return lax.dot_general(a, b, NT, preferred_element_type=jnp.float32)


def loop(low, high, body):
    if high - low <= 4:
        for i in range(low, high):
            body(i)
    else:
        def step(i, carry):
            body(i)
            return carry
        lax.fori_loop(low, high, step, 0)


def kernel(
    nd, nt, seq_len, scale,
    lengths, acts, grads, pin, pout, query, pre_in, pre_out,
    out,
    acts_v, grads_v, pin_v, pout_v, query_v, pre_in_v, pre_out_v,
    part, got, gather, rows, final,
    load_sem, send_a, recv_a, send_b, recv_b, send_c, recv_c,
):
    d = lax.axis_index("dp")
    t = lax.axis_index("tensor")
    width = pin.shape[0]
    half = width // 2
    tok = acts.shape[0] // nt
    count = out.shape[0]
    nq = query.shape[0]
    total = nd * nt

    def place(k):
        chips = nt // 2
        return ((t // 2 + chips - 1 - k // 2) % chips) * 2 + (t % 2 + 1 - k % 2) % 2

    barrier = pltpu.get_barrier_semaphore()

    def greet(name, place, size):
        def one(i):
            pl.semaphore_signal(barrier, inc=1, device_id={name: (place + i) % size}, device_id_type=MESH)
        loop(1, size, one)

    greet("dp", d, nd)
    greet("tensor", t, nt)

    fixed = [
        pltpu.make_async_copy(src, dst, load_sem.at[2 * nt + i])
        for i, (src, dst) in enumerate(
            [(pre_in, pre_in_v), (pre_out, pre_out_v), (pin, pin_v), (pout, pout_v), (query, query_v)]
        )
    ]
    for copy in fixed[:4]:
        copy.start()
    loads = []
    for k in range(nt):
        chunk = pl.ds(pl.multiple_of(place(k) * tok, tok), tok)
        loads.append((
            pltpu.make_async_copy(acts.at[chunk, :], acts_v.at[k], load_sem.at[2 * k]),
            pltpu.make_async_copy(grads.at[chunk, :], grads_v.at[k], load_sem.at[2 * k + 1]),
        ))
        for copy in loads[k]:
            copy.start()
    fixed[4].start()

    for copy in fixed[:2]:
        copy.wait()
    r = lax.broadcasted_iota(jnp.int32, (width, width), 0)
    c = lax.broadcasted_iota(jnp.int32, (width, width), 1)
    pick = jnp.where(c == jnp.where(r < half, 2 * r, 2 * (r - half) + 1), 1.0, 0.0).astype(jnp.float32)
    pre_t = f32dot(pick, pre_in_v[...], NT)

    for copy in fixed[2:4]:
        copy.wait()
    sends = []
    for k in range(nt):
        for copy in loads[k]:
            copy.wait()
        part[k, 0:width, 0:tok] = bf16dot(pin_v[...], acts_v[k])
        part[k, 0:tok, tok : tok + width] = bf16dot(grads_v[k], pout_v[...])
        if k == 1:
            pl.semaphore_wait(barrier, nd + nt - 2)
        if k < nt - 1:
            copy = pltpu.make_async_remote_copy(
                src_ref=part.at[k], dst_ref=got.at[k], send_sem=send_a.at[k], recv_sem=recv_a.at[k],
                device_id={"tensor": place(k)}, device_id_type=MESH,
            )
            sends.append(copy)
        if k >= 1:
            for copy in sends[0 if k == 1 else k : k + 1]:
                copy.start()
    fixed[4].wait()

    left = part[nt - 1, 0:width, 0:tok]
    right = part[nt - 1, 0:tok, tok : tok + width]
    for k in range(nt - 2, -1, -1):
        sends[k].wait_recv()
        left = left + got[k, 0:width, 0:tok]
        right = right + got[k, 0:tok, tok : tok + width]
    start = t * tok
    length = lengths[start // seq_len]
    slot = lax.broadcasted_iota(jnp.int32, (width, tok), 1) + start % seq_len
    left = jnp.where(slot < length, left, 0.0)
    u = split_dot(pre_t, left, NN)
    w = split_dot(right, pre_out_v[...], NT)
    g = split_dot(u, w, NN)
    gather[0] = jnp.concatenate([g[:half], g[half:]], axis=1)

    def gather_copy(j):
        return pltpu.make_async_remote_copy(
            src_ref=gather.at[0], dst_ref=gather.at[j], send_sem=send_b.at[j], recv_sem=recv_b.at[j],
            device_id={"dp": (d + j) % nd}, device_id_type=MESH,
        )

    loop(1, nd, lambda j: gather_copy(j).start())

    ones = jnp.ones((8, 2 * width), jnp.bfloat16)
    mine = d * nt + t

    def score(j):
        acc = jnp.zeros((nq, 2 * width), jnp.float32)
        for p in range(half):
            acc = acc + query_v[:, 2 * width * p : 2 * width * (p + 1)] * gather[j, p : p + 1, :]
        high, low = halves(acc)
        row = (bf16dot(ones, high) + bf16dot(ones, low))[0:1] * scale
        rows[j] = jnp.concatenate([row, row], axis=1)

    def row_copy(j, to):
        return pltpu.make_async_remote_copy(
            src_ref=rows.at[j], dst_ref=final.at[mine], send_sem=send_c, recv_sem=recv_c,
            device_id={"dp": (d + nd - j) % nd, "tensor": to}, device_id_type=MESH,
        )

    score(0)
    final[mine] = rows[0]
    loop(1, nt, lambda k: row_copy(0, (t + k) % nt).start())

    def step(j):
        gather_copy(j).wait_recv()
        score(j)
        loop(0, nt, lambda k: row_copy(j, (t + k) % nt).start())

    loop(1, nd, step)

    for copy in sends:
        copy.wait_send()
    loop(1, nd, lambda j: gather_copy(j).wait_send())
    most = final.at[pl.ds(0, total - 1)]
    pltpu.make_async_copy(most, most, send_c).wait()
    pltpu.make_async_copy(most, most, recv_c).wait()

    share = nt // count
    lane = lax.broadcasted_iota(jnp.int32, (1, 2 * nq), 1)
    for s in range(count):
        for pair in range(nd // 2):
            sums = []
            for e in range(2):
                base = (2 * pair + e) * nt + s * share
                value = final[base]
                for i in range(1, share):
                    value = value + final[base + i]
                sums.append(value)
            out[s : s + 1, 2 * nq * pair : 2 * nq * (pair + 1)] = jnp.where(lane < nq, sums[0], sums[1])


def solution(mesh):
    nd, nt = mesh.shape["dp"], mesh.shape["tensor"]

    def local(acts, grads, lengths, pin, pout, query, pre_in, pre_out):
        tokens, deep_in = acts.shape
        deep_out = grads.shape[1]
        count = lengths.shape[0]
        width = pin.shape[1]
        nq = query.shape[0]
        tok = tokens // nt
        seq_len = tokens // count
        scale = 1.0 / math.sqrt(seq_len) / math.sqrt(width * width)
        box = (max(width, tok), tok + width)
        anywhere = pl.BlockSpec(memory_space=pltpu.HBM)
        f32 = jnp.float32
        dma = pltpu.SemaphoreType.DMA
        return pl.pallas_call(
            functools.partial(kernel, nd, nt, seq_len, scale),
            out_shape=jax.ShapeDtypeStruct((count, nd * nq), f32),
            in_specs=[pl.BlockSpec(memory_space=pltpu.SMEM)] + [anywhere] * 7,
            out_specs=pl.BlockSpec(memory_space=pltpu.VMEM),
            scratch_shapes=[
                pltpu.VMEM((nt, tok, deep_in), acts.dtype),
                pltpu.VMEM((nt, tok, deep_out), grads.dtype),
                pltpu.VMEM((width, deep_in), pin.dtype),
                pltpu.VMEM((width, deep_out), pout.dtype),
                pltpu.VMEM(query.shape, f32),
                pltpu.VMEM(pre_in.shape, f32),
                pltpu.VMEM(pre_out.shape, f32),
                pltpu.VMEM((nt,) + box, f32),
                pltpu.VMEM((nt - 1,) + box, f32),
                pltpu.VMEM((nd, width // 2, 2 * width), f32),
                pltpu.VMEM((nd, 1, 2 * nq), f32),
                pltpu.VMEM((nd * nt, 1, 2 * nq), f32),
                dma((2 * nt + 5,)), dma((nt - 1,)), dma((nt - 1,)), dma((nd,)), dma((nd,)), dma, dma,
            ],
            compiler_params=pltpu.CompilerParams(
                collective_id=0, has_side_effects=True, vmem_limit_bytes=60 * 1024 * 1024
            ),
        )(lengths, acts, grads, pin.T, pout.T, query, pre_in, pre_out)

    placed = (
        P(("groups", "dp"), "tensor"),
        P(("groups", "dp"), "tensor"),
        P(("groups", "dp")),
        P("tensor", None),
        P("tensor", None),
        P(("groups", "dp"), None),
        P(),
        P(),
    )
    return jax.shard_map(
        local, mesh=mesh, in_specs=placed, out_specs=P(("groups", "dp"), None), check_vma=False
    )
```
